32 devices in a mesh: ctx: 8 (over z, y), mp: 4 (over x, core).
Axes of the slice: x: 2, y: 2, z: 4, core: 2. Of those that a mesh axis runs over, the one named last changes fastest.
Arguments:
- queries: bfloat16 [2, 1536, 5120], P(None, 'ctx', 'mp'), may hold values from -24 to 24
- cache_keys: bfloat16 [1536, 5120], P(('ctx', 'mp')), may hold values from -26 to 26
- cache_values: bfloat16 [1536, 5120], P(('ctx', 'mp')), may hold values from -6 to 6
- douts: bfloat16 [2, 1536, 5120], P(None, 'ctx', 'mp'), may hold values from -6 to 6
- reads: int32 [8, 24], P('ctx'), may hold values from -1 to 95, as said below
Outputs:
- attn_out: bfloat16 [2, 1536, 5120], P(None, 'ctx', 'mp')
- d_queries: bfloat16 [2, 1536, 5120], P(None, 'ctx', 'mp')
- d_cache_keys: float32 [1536, 5120], P(('ctx', 'mp'))
- d_cache_values: float32 [1536, 5120], P(('ctx', 'mp'))
The draws below stay inside these ranges and needn't reach their ends.
Inputs may be any that keep to these rules, and one draw needn't show every extreme that they name: Row c names, in rising order, the blocks that stretch c reads, then -1 in the remaining slots. Every named block ends at or before stretch c's last position. Block 0 is named in every row. Owner o holds blocks 3 * o to 3 * o + 2; a row names at most one block of an owner, and exactly one of each of the 4 owners of stretch c's own positions. Row c names min(24, 4 * (c + 1)) blocks.
All inputs are finite; a program needn't handle non-finite values.
Results may differ from the reference program's by a relative error of at most 0.017.
Values may be sent and summed in bfloat16 or wider, within the bound.
A program may use at most 256 MiB of HBM per device.

```python
import math
import jax
import jax.numpy as jnp
from jax import lax

HEADS = 40
HD = 128
LAYERS = 2
BLK = 16
TOK_DEV = 192
STRETCHES = 8
OWNERS = 32
SEQ = 1536
BPD = 3
READS = 24
N_MP = 4


def chosen_reads(key):
    folded = jax.random.fold_in(key, 101)
    key_rank, key_block = jax.random.split(folded)
    owners = jnp.arange(OWNERS, dtype=jnp.int32)
    stretches = jnp.arange(STRETCHES, dtype=jnp.int32)[:, None]
    home_stretch = owners[None, :] // N_MP
    forced = (home_stretch == stretches) | (owners[None, :] == 0)
    reach = home_stretch <= stretches
    rank_noise = jax.random.randint(key_rank, (STRETCHES, OWNERS), 0, 1 << 16) * OWNERS + owners[None, :]
    beyond_score = (1 << 16) * OWNERS + owners[None, :]
    rank_score = jnp.where(forced, owners[None, :] - OWNERS, jnp.where(reach, rank_noise, beyond_score))
    owner_rank = jnp.argsort(jnp.argsort(rank_score, axis=1), axis=1)
    read_count = jnp.minimum(READS, N_MP * (stretches + 1))
    picked = owner_rank < read_count
    local_block = jax.random.randint(key_block, (STRETCHES, OWNERS), 0, BPD)
    local_block = jnp.where(owners[None, :] == 0, 0, local_block)
    block_ids = owners[None, :] * BPD + local_block
    beyond = OWNERS * BPD
    listed = jnp.sort(jnp.where(picked, block_ids, beyond), axis=1)[:, :READS]
    return jnp.where(listed == beyond, -1, listed).astype(jnp.int32)


def draw_reads(key, part):
    listed = chosen_reads(key)
    return listed


def draw_cache_keys(key, part):
    drawn = jax.random.normal(jax.random.fold_in(key, 109), (SEQ, HEADS * HD), jnp.float32)
    drawn = jnp.clip(drawn, -6.0, 6.0)
    return drawn.astype(jnp.bfloat16)


def draw_queries(key, part):
    drawn = jax.random.normal(jax.random.fold_in(key, 127), (LAYERS, SEQ, HEADS * HD), jnp.float32)
    drawn = jnp.clip(drawn, -6.0, 6.0)
    return drawn.astype(jnp.bfloat16)


def shard_levels(key, shape, cuts, low, largest):
    gain = 1.0
    for dim, shards_of in cuts:
        steps = jax.random.uniform(jax.random.fold_in(jax.random.fold_in(key, 6), dim), (shards_of,), jnp.float32, low / len(cuts), largest / len(cuts))
        gain = gain * jnp.repeat(jnp.exp(steps), shape[dim] // shards_of).reshape((-1,) + (1,) * (len(shape) - 1 - dim))
    return gain


def noise(own_key, extent, spread, most, shards=(), held_as=jnp.bfloat16):
    values = jax.random.normal(own_key, extent, jnp.float32) * spread
    if len(shards) > 0:
        values = shard_levels(own_key, extent, shards, -0.22, 0.18) * values
    return jnp.clip(values, min=-most, max=most).astype(held_as)


def setup_inputs(seed: int = 0) -> dict:
    splits = jax.random.split(jax.random.key(seed), 6)
    return {
        "queries": draw_queries(jax.random.fold_in(splits[5], 71), 0),
        "cache_keys": draw_cache_keys(jax.random.fold_in(splits[5], 71), 0),
        "cache_values": noise(splits[2], (SEQ, HEADS * HD), 1.0, 6.0, ((0, 32),)),
        "douts": noise(splits[3], (LAYERS, SEQ, HEADS * HD), 1.0, 6.0, ((1, 8), (2, 4))),
        "reads": draw_reads(jax.random.fold_in(splits[5], 71), 0),
    }


neg_big = -1e+30

def reference(queries, cache_keys, cache_values, douts, reads):
    factor = 1.0 / math.sqrt(HD)
    offsets = jnp.arange(BLK, dtype=jnp.int32)
    rows_here = jnp.arange(TOK_DEV, dtype=jnp.int32)

    def one_stretch(running, stretch_id):
        grad_keys, grad_values = running
        listed = lax.dynamic_index_in_dim(reads, stretch_id, 0, keepdims=False)
        in_use = listed >= 0
        clamped = jnp.where(in_use, listed, 0).astype(jnp.int32)
        key_pos = (clamped[:, None] * BLK + offsets[None, :]).reshape(-1).astype(jnp.int32)
        key_live = jnp.repeat(in_use, BLK)
        query_pos = stretch_id * TOK_DEV + rows_here
        visible = key_live[None, :] & (key_pos[None, :] <= query_pos[:, None])
        key_rows = cache_keys[key_pos].astype(jnp.float32).reshape(-1, HEADS, HD)
        value_rows = cache_values[key_pos].astype(jnp.float32).reshape(-1, HEADS, HD)
        key_sum = jnp.zeros(key_rows.shape, jnp.float32)
        value_sum = jnp.zeros(value_rows.shape, jnp.float32)
        outs_here = []
        grads_here = []
        for layer_id in range(LAYERS):
            query_rows = lax.dynamic_slice_in_dim(queries[layer_id], stretch_id * TOK_DEV, TOK_DEV, 0)
            query_rows = query_rows.astype(jnp.float32).reshape(TOK_DEV, HEADS, HD)
            dout_rows = lax.dynamic_slice_in_dim(douts[layer_id], stretch_id * TOK_DEV, TOK_DEV, 0)
            dout_rows = dout_rows.astype(jnp.float32).reshape(TOK_DEV, HEADS, HD)
            scores = jnp.einsum('qhd,khd->hqk', query_rows, key_rows) * factor
            scores = jnp.where(visible[None], scores, neg_big)
            row_top = lax.optimization_barrier(jnp.max(scores, axis=2, keepdims=True))
            raised = jnp.exp(scores - row_top)
            prob_full = raised / lax.optimization_barrier(jnp.sum(raised, axis=2, keepdims=True))
            probs_low = lax.optimization_barrier(prob_full.astype(jnp.bfloat16)).astype(jnp.float32)
            attended = jnp.einsum('hqk,khd->qhd', probs_low, value_rows).astype(jnp.bfloat16)
            row_delta = lax.optimization_barrier(jnp.sum(dout_rows * attended.astype(jnp.float32), axis=2))
            d_probs = jnp.einsum('qhd,khd->hqk', dout_rows, value_rows)
            d_scores = prob_full * (d_probs - row_delta.T[:, :, None])
            d_scores = lax.optimization_barrier(d_scores.astype(jnp.bfloat16)).astype(jnp.float32)
            d_query = (jnp.einsum('hqk,khd->qhd', d_scores, key_rows) * factor).astype(jnp.bfloat16)
            key_sum = key_sum + jnp.einsum('hqk,qhd->khd', d_scores, query_rows) * factor
            value_sum = value_sum + jnp.einsum('hqk,qhd->khd', probs_low, dout_rows)
            outs_here.append(attended.reshape(TOK_DEV, HEADS * HD))
            grads_here.append(d_query.reshape(TOK_DEV, HEADS * HD))
        grad_keys = grad_keys.at[key_pos].add(key_sum.reshape(-1, HEADS * HD))
        grad_values = grad_values.at[key_pos].add(value_sum.reshape(-1, HEADS * HD))
        return ((grad_keys, grad_values), (jnp.stack(outs_here), jnp.stack(grads_here)))
    start = (jnp.zeros((SEQ, HEADS * HD), jnp.float32), jnp.zeros((SEQ, HEADS * HD), jnp.float32))
    finals, stacked = lax.scan(one_stretch, start, jnp.arange(STRETCHES, dtype=jnp.int32))
    attn_out = stacked[0].transpose(1, 0, 2, 3).reshape(LAYERS, SEQ, HEADS * HD)
    d_queries = stacked[1].transpose(1, 0, 2, 3).reshape(LAYERS, SEQ, HEADS * HD)
    return (attn_out, d_queries, finals[0], finals[1])
```

```python
import functools
import math

import jax
import jax.numpy as jnp
from jax import lax
from jax.experimental import pallas as pl
from jax.experimental.pallas import tpu as pltpu
from jax.sharding import PartitionSpec as P

HD = 128
BLK = 16
LANES = 128
MESH = pl.DeviceIdType.MESH
FAR = 1e9
LOW = -1e30


def rows_by(a, b):
    return lax.dot_general(a, b, (((1,), (1,)), ((), ())), preferred_element_type=jnp.float32)


def plain(a, b):
    return lax.dot_general(a, b, (((1,), (0,)), ((), ())), preferred_element_type=jnp.float32)


def over_rows(a, b):
    return lax.dot_general(a, b, (((0,), (0,)), ((), ())), preferred_element_type=jnp.float32)


def kernel(
    sizes,
    q_ref,
    k_ref,
    v_ref,
    do_ref,
    list_ref,
    o_ref,
    dq_ref,
    dk_ref,
    dv_ref,
    out_blocks,
    kv_blocks,
    grad_blocks,
    lists,
    hits,
    bias,
    list_send,
    list_recv,
    kv_send,
    kv_recv,
    grad_send,
    grad_recv,
):
    ctx_n, mp_n, chunks, width = sizes
    layers, tok, head_width = q_ref.shape
    per_owner = k_ref.shape[0] // BLK
    owners = ctx_n * mp_n
    keys = owners * BLK
    factor = 1.0 / math.sqrt(HD)
    my_c = lax.axis_index("ctx")
    my_m = lax.axis_index("mp")
    owner = my_c * mp_n + my_m

    def columns(m, ch):
        return pl.ds(pl.multiple_of(m * head_width + ch * width, LANES), width)

    def loop(low, high, body):
        def step(i, carry):
            body(i)
            return carry

        lax.fori_loop(low, high, step, 0)

    def wait_bytes(ref, sem):
        pltpu.make_async_copy(ref, ref, sem).wait()

    def clear(ch):
        kv_blocks[ch] = jnp.zeros(kv_blocks.shape[1:], kv_blocks.dtype)

    loop(0, chunks, clear)
    lists[...] = jnp.full(lists.shape, -1, jnp.int32)
    lists[my_c] = list_ref[...]

    barrier = pltpu.get_barrier_semaphore()

    def greet(t):
        @pl.when(t != owner)
        def _():
            pl.semaphore_signal(
                barrier, inc=1, device_id=(t // mp_n, t % mp_n), device_id_type=MESH
            )

    loop(0, owners, greet)
    pl.semaphore_wait(barrier, owners - 1)

    def send_list(c):
        pltpu.make_async_remote_copy(
            src_ref=list_ref,
            dst_ref=lists.at[my_c],
            send_sem=list_send.at[c],
            recv_sem=list_recv.at[my_c],
            device_id=(c, my_m),
            device_id_type=MESH,
        ).start()

    loop(0, my_c, send_list)

    named = list_ref[...].T[:, 0:1]
    lane = lax.broadcasted_iota(jnp.int32, (named.shape[0], keys), 1)
    first = (lane >> 4) * per_owner
    hit = (named >= first) & (named < first + per_owner)
    key_pos = jnp.sum(
        jnp.where(hit, (named * BLK + (lane & (BLK - 1))).astype(jnp.float32), 0.0),
        axis=0,
        keepdims=True,
    )
    live = jnp.sum(jnp.where(hit, 1.0, 0.0), axis=0, keepdims=True)
    key_pos = jnp.where(live > 0.5, key_pos, FAR)
    query_pos = (my_c * tok + lax.broadcasted_iota(jnp.int32, (tok, keys), 0)).astype(jnp.float32)
    bias[...] = jnp.where(key_pos <= query_pos, 0.0, LOW)

    loop(my_c + 1, ctx_n, lambda c: wait_bytes(lists.at[c], list_recv.at[c]))
    rows = lists[:, 0, :]
    for b in range(per_owner):
        found = jnp.sum(
            jnp.where(rows == owner * per_owner + b, 1.0, 0.0), axis=1, keepdims=True
        )
        hits[b] = jnp.broadcast_to(found, (ctx_n, width))

    def send_chunk(ch):
        def to_stretch(step):
            c = ctx_n - 1 - step
            wanted = [hits[b, pl.ds(c, 1), :] for b in range(per_owner)]
            for i in range(mp_n):
                m = lax.rem(my_m + i, mp_n)
                cols = columns(m, ch)
                for part, source in enumerate((k_ref, v_ref)):
                    picked = source[0:BLK, cols].astype(jnp.float32) * wanted[0]
                    for b in range(1, per_owner):
                        block = source[b * BLK : (b + 1) * BLK, cols].astype(jnp.float32)
                        picked = picked + block * wanted[b]
                    out_blocks[ch, c, m, part] = picked.astype(jnp.bfloat16)

                def away(m=m):
                    pltpu.make_async_remote_copy(
                        src_ref=out_blocks.at[ch, c, m],
                        dst_ref=kv_blocks.at[ch, :, owner],
                        send_sem=kv_send.at[ch, c],
                        recv_sem=kv_recv.at[ch, my_c],
                        device_id=(c, m),
                        device_id_type=MESH,
                    ).start()

                if i > 0:
                    away()
                else:
                    pl.when(c != my_c)(away)

                    @pl.when(c == my_c)
                    def _(m=m):
                        pltpu.make_async_copy(
                            out_blocks.at[ch, c, m],
                            kv_blocks.at[ch, :, owner],
                            kv_recv.at[ch, my_c],
                        ).start()

        loop(0, ctx_n - my_c, to_stretch)

    loop(0, chunks, send_chunk)

    def work_chunk(ch):
        loop(
            0,
            my_c + 1,
            lambda s: wait_bytes(
                kv_blocks.at[ch, :, pl.ds(s * mp_n, mp_n)], kv_recv.at[ch, s]
            ),
        )
        for h in range(width // HD):
            here = slice(h * HD, (h + 1) * HD)
            cols = pl.ds(pl.multiple_of(ch * width + h * HD, LANES), HD)
            key_rows = kv_blocks[ch, 0, :, :, here].reshape(keys, HD)
            value_rows = kv_blocks[ch, 1, :, :, here].reshape(keys, HD)
            query_rows = q_ref[:, :, cols].reshape(layers * tok, HD)
            dout_rows = do_ref[:, :, cols].reshape(layers * tok, HD)
            scores = rows_by(query_rows, key_rows) * factor
            scores = (scores.reshape(layers, tok, keys) + bias[...][None]).reshape(
                layers * tok, keys
            )
            raised = jnp.exp(scores - jnp.max(scores, axis=1, keepdims=True))
            probs = raised * (1.0 / jnp.sum(raised, axis=1, keepdims=True))
            probs_low = probs.astype(jnp.bfloat16)
            attended = plain(probs_low, value_rows).astype(jnp.bfloat16)
            delta = jnp.sum(
                dout_rows.astype(jnp.float32) * attended.astype(jnp.float32),
                axis=1,
                keepdims=True,
            )
            d_probs = rows_by(dout_rows, value_rows)
            d_scores = (probs * (d_probs - delta)).astype(jnp.bfloat16)
            o_ref[:, :, cols] = attended.reshape(layers, tok, HD)
            d_query = (plain(d_scores, key_rows) * factor).astype(jnp.bfloat16)
            dq_ref[:, :, cols] = d_query.reshape(layers, tok, HD)
            d_keys = (over_rows(d_scores, query_rows) * factor).astype(jnp.bfloat16)
            d_values = over_rows(probs_low, dout_rows).astype(jnp.bfloat16)
            kv_blocks[ch, 0, :, :, here] = d_keys.reshape(owners, BLK, HD)
            kv_blocks[ch, 1, :, :, here] = d_values.reshape(owners, BLK, HD)

        def to_owners(s):
            for i in range(mp_n):
                m = lax.rem(my_m + i, mp_n)

                def away(m=m):
                    pltpu.make_async_remote_copy(
                        src_ref=kv_blocks.at[ch, :, s * mp_n + m],
                        dst_ref=grad_blocks.at[ch, my_c, my_m],
                        send_sem=grad_send.at[ch, s],
                        recv_sem=grad_recv.at[ch, my_c],
                        device_id=(s, m),
                        device_id_type=MESH,
                    ).start()

                if i > 0:
                    away()
                else:
                    pl.when(s != my_c)(away)

                    @pl.when(s == my_c)
                    def _():
                        pltpu.make_async_copy(
                            kv_blocks.at[ch, :, owner],
                            grad_blocks.at[ch, my_c, my_m],
                            grad_recv.at[ch, my_c],
                        ).start()

        loop(0, my_c + 1, to_owners)

    loop(0, chunks, work_chunk)

    dk_ref[...] = jnp.zeros(dk_ref.shape, jnp.float32)
    dv_ref[...] = jnp.zeros(dv_ref.shape, jnp.float32)

    def absorb_chunk(ch):
        def from_stretch(c):
            wait_bytes(grad_blocks.at[ch, c], grad_recv.at[ch, c])
            wanted = [hits[b, pl.ds(c, 1), :] for b in range(per_owner)]
            for m in range(mp_n):
                cols = columns(m, ch)
                for part, target in enumerate((dk_ref, dv_ref)):
                    grad = grad_blocks[ch, c, m, part].astype(jnp.float32)
                    for b in range(per_owner):
                        target[b * BLK : (b + 1) * BLK, cols] += grad * wanted[b]

        loop(my_c, ctx_n, from_stretch)

    loop(0, chunks, absorb_chunk)

    loop(0, my_c, lambda c: wait_bytes(list_ref, list_send.at[c]))

    def finish(ch):
        loop(my_c + 1, ctx_n, lambda c: wait_bytes(out_blocks.at[ch, c], kv_send.at[ch, c]))
        wait_bytes(out_blocks.at[ch, my_c, pl.ds(0, mp_n - 1)], kv_send.at[ch, my_c])
        loop(
            0,
            my_c,
            lambda s: wait_bytes(
                kv_blocks.at[ch, :, pl.ds(s * mp_n, mp_n)], grad_send.at[ch, s]
            ),
        )
        wait_bytes(kv_blocks.at[ch, :, pl.ds(my_c * mp_n, mp_n - 1)], grad_send.at[ch, my_c])

    loop(0, chunks, finish)


def on_device(queries, cache_keys, cache_values, douts, reads):
    layers, tok, head_width = queries.shape
    kv_rows, full_width = cache_keys.shape
    ctx_n = lax.axis_size("ctx")
    mp_n = lax.axis_size("mp")
    per_owner = kv_rows // BLK
    owners = ctx_n * mp_n
    heads = head_width // HD
    per_chunk = 2 if heads % 2 == 0 else 1
    chunks = heads // per_chunk
    width = per_chunk * HD
    slots = reads.shape[1]
    padded = -(-slots // LANES) * LANES
    listed = jnp.pad(reads, ((0, 7), (0, padded - slots)), constant_values=-1)
    vmem = pl.BlockSpec(memory_space=pltpu.VMEM)
    dma = pltpu.SemaphoreType.DMA
    return pl.pallas_call(
        functools.partial(kernel, (ctx_n, mp_n, chunks, width)),
        out_shape=(
            jax.ShapeDtypeStruct(queries.shape, jnp.bfloat16),
            jax.ShapeDtypeStruct(queries.shape, jnp.bfloat16),
            jax.ShapeDtypeStruct(cache_keys.shape, jnp.float32),
            jax.ShapeDtypeStruct(cache_values.shape, jnp.float32),
        ),
        in_specs=[vmem] * 5,
        out_specs=(vmem,) * 4,
        scratch_shapes=[
            pltpu.VMEM((chunks, ctx_n, mp_n, 2, BLK, width), jnp.bfloat16),
            pltpu.VMEM((chunks, 2, owners, BLK, width), jnp.bfloat16),
            pltpu.VMEM((chunks, ctx_n, mp_n, 2, BLK, width), jnp.bfloat16),
            pltpu.VMEM((ctx_n, 8, padded), jnp.int32),
            pltpu.VMEM((per_owner, ctx_n, width), jnp.float32),
            pltpu.VMEM((tok, owners * BLK), jnp.float32),
            dma((ctx_n,)),
            dma((ctx_n,)),
            dma((chunks, ctx_n)),
            dma((chunks, ctx_n)),
            dma((chunks, ctx_n)),
            dma((chunks, ctx_n)),
        ],
        compiler_params=pltpu.CompilerParams(
            collective_id=0, has_side_effects=True, vmem_limit_bytes=60 * 1024 * 1024
        ),
    )(queries, cache_keys, cache_values, douts, listed)


def solution(mesh):
    return jax.shard_map(
        on_device,
        mesh=mesh,
        in_specs=(
            P(None, "ctx", "mp"),
            P(("ctx", "mp"), None),
            P(("ctx", "mp"), None),
            P(None, "ctx", "mp"),
            P("ctx", None),
        ),
        out_specs=(
            P(None, "ctx", "mp"),
            P(None, "ctx", "mp"),
            P(("ctx", "mp"), None),
            P(("ctx", "mp"), None),
        ),
        check_vma=False,
    )
```

```python
import functools
import math

import jax
import jax.numpy as jnp
from jax import lax
from jax.experimental import pallas as pl
from jax.experimental.pallas import tpu as pltpu
from jax.sharding import PartitionSpec as P

HD = 128
BLK = 16
LANES = 128
MESH = pl.DeviceIdType.MESH
FAR = 1e9
LOW = -1e30


def rows_by(a, b):
    return lax.dot_general(a, b, (((1,), (1,)), ((), ())), preferred_element_type=jnp.float32)


def plain(a, b):
    return lax.dot_general(a, b, (((1,), (0,)), ((), ())), preferred_element_type=jnp.float32)


def over_rows(a, b):
    return lax.dot_general(a, b, (((0,), (0,)), ((), ())), preferred_element_type=jnp.float32)


def kernel(
    sizes,
    q_ref,
    k_ref,
    v_ref,
    do_ref,
    reads_ref,
    o_ref,
    dq_ref,
    dk_ref,
    dv_ref,
    out_blocks,
    kv_blocks,
    grad_blocks,
    list_ref,
    lists,
    hits,
    bias,
    list_send,
    list_recv,
    kv_send,
    kv_recv,
    grad_send,
    grad_recv,
):
    ctx_n, mp_n, chunks, width = sizes
    layers, tok, head_width = q_ref.shape
    per_owner = k_ref.shape[0] // BLK
    owners = ctx_n * mp_n
    keys = owners * BLK
    factor = 1.0 / math.sqrt(HD)
    my_c = lax.axis_index("ctx")
    my_m = lax.axis_index("mp")
    owner = my_c * mp_n + my_m

    def columns(m, ch):
        return pl.ds(pl.multiple_of(m * head_width + ch * width, LANES), width)

    def loop(low, high, body):
        def step(i, carry):
            body(i)
            return carry

        lax.fori_loop(low, high, step, 0)

    def wait_bytes(ref, sem):
        pltpu.make_async_copy(ref, ref, sem).wait()

    def clear(ch):
        kv_blocks[ch] = jnp.zeros(kv_blocks.shape[1:], kv_blocks.dtype)

    loop(0, chunks, clear)
    list_ref[...] = jnp.full(list_ref.shape, -1, jnp.int32)
    list_ref[0:1, 0 : reads_ref.shape[1]] = reads_ref[...]
    lists[...] = jnp.full(lists.shape, -1, jnp.int32)
    lists[my_c] = list_ref[...]

    barrier = pltpu.get_barrier_semaphore()

    def greet(t):
        @pl.when(t != owner)
        def _():
            pl.semaphore_signal(
                barrier, inc=1, device_id=(t // mp_n, t % mp_n), device_id_type=MESH
            )

    loop(0, owners, greet)
    pl.semaphore_wait(barrier, owners - 1)

    def send_list(c):
        pltpu.make_async_remote_copy(
            src_ref=list_ref,
            dst_ref=lists.at[my_c],
            send_sem=list_send.at[c],
            recv_sem=list_recv.at[my_c],
            device_id=(c, my_m),
            device_id_type=MESH,
        ).start()

    loop(0, my_c, send_list)

    named = list_ref[...].T[:, 0:1]
    lane = lax.broadcasted_iota(jnp.int32, (named.shape[0], keys), 1)
    first = (lane >> 4) * per_owner
    hit = (named >= first) & (named < first + per_owner)
    key_pos = jnp.sum(
        jnp.where(hit, (named * BLK + (lane & (BLK - 1))).astype(jnp.float32), 0.0),
        axis=0,
        keepdims=True,
    )
    live = jnp.sum(jnp.where(hit, 1.0, 0.0), axis=0, keepdims=True)
    key_pos = jnp.where(live > 0.5, key_pos, FAR)
    query_pos = (my_c * tok + lax.broadcasted_iota(jnp.int32, (tok, keys), 0)).astype(jnp.float32)
    bias[...] = jnp.where(key_pos <= query_pos, 0.0, LOW)

    loop(my_c + 1, ctx_n, lambda c: wait_bytes(lists.at[c], list_recv.at[c]))
    rows = lists[:, 0, :]
    for b in range(per_owner):
        found = jnp.sum(
            jnp.where(rows == owner * per_owner + b, 1.0, 0.0), axis=1, keepdims=True
        )
        hits[b] = jnp.broadcast_to(found, (ctx_n, width))

    def send_chunk(ch):
        def to_stretch(step):
            c = ctx_n - 1 - step
            wanted = [hits[b, pl.ds(c, 1), :] for b in range(per_owner)]
            for i in range(mp_n):
                m = lax.rem(my_m + i, mp_n)
                cols = columns(m, ch)
                for part, source in enumerate((k_ref, v_ref)):
                    picked = source[0:BLK, cols].astype(jnp.float32) * wanted[0]
                    for b in range(1, per_owner):
                        block = source[b * BLK : (b + 1) * BLK, cols].astype(jnp.float32)
                        picked = picked + block * wanted[b]
                    out_blocks[ch, c, m, part] = picked.astype(jnp.bfloat16)

                def away(m=m):
                    pltpu.make_async_remote_copy(
                        src_ref=out_blocks.at[ch, c, m],
                        dst_ref=kv_blocks.at[ch, owner],
                        send_sem=kv_send.at[ch, c],
                        recv_sem=kv_recv.at[ch, my_c],
                        device_id=(c, m),
                        device_id_type=MESH,
                    ).start()

                if i > 0:
                    away()
                else:
                    pl.when(c != my_c)(away)

                    @pl.when(c == my_c)
                    def _(m=m):
                        pltpu.make_async_copy(
                            out_blocks.at[ch, c, m],
                            kv_blocks.at[ch, owner],
                            kv_recv.at[ch, my_c],
                        ).start()

        loop(0, ctx_n - my_c, to_stretch)

    loop(0, chunks, send_chunk)

    def work_chunk(ch):
        loop(
            0,
            my_c + 1,
            lambda s: wait_bytes(
                kv_blocks.at[ch, pl.ds(s * mp_n, mp_n)], kv_recv.at[ch, s]
            ),
        )
        for h in range(width // HD):
            here = slice(h * HD, (h + 1) * HD)
            cols = pl.ds(pl.multiple_of(ch * width + h * HD, LANES), HD)
            key_rows = kv_blocks[ch, :, 0, :, here].reshape(keys, HD)
            value_rows = kv_blocks[ch, :, 1, :, here].reshape(keys, HD)
            query_rows = q_ref[:, :, cols].reshape(layers * tok, HD)
            dout_rows = do_ref[:, :, cols].reshape(layers * tok, HD)
            scores = rows_by(query_rows, key_rows) * factor
            scores = (scores.reshape(layers, tok, keys) + bias[...][None]).reshape(
                layers * tok, keys
            )
            raised = jnp.exp(scores - jnp.max(scores, axis=1, keepdims=True))
            probs = raised * (1.0 / jnp.sum(raised, axis=1, keepdims=True))
            probs_low = probs.astype(jnp.bfloat16)
            attended = plain(probs_low, value_rows).astype(jnp.bfloat16)
            delta = jnp.sum(
                dout_rows.astype(jnp.float32) * attended.astype(jnp.float32),
                axis=1,
                keepdims=True,
            )
            d_probs = rows_by(dout_rows, value_rows)
            d_scores = (probs * (d_probs - delta)).astype(jnp.bfloat16)
            o_ref[:, :, cols] = attended.reshape(layers, tok, HD)
            d_query = (plain(d_scores, key_rows) * factor).astype(jnp.bfloat16)
            dq_ref[:, :, cols] = d_query.reshape(layers, tok, HD)
            d_keys = (over_rows(d_scores, query_rows) * factor).astype(jnp.bfloat16)
            d_values = over_rows(probs_low, dout_rows).astype(jnp.bfloat16)
            kv_blocks[ch, :, 0, :, here] = d_keys.reshape(owners, BLK, HD)
            kv_blocks[ch, :, 1, :, here] = d_values.reshape(owners, BLK, HD)

        def to_owners(s):
            for i in range(mp_n):
                m = lax.rem(my_m + i, mp_n)

                def away(m=m):
                    pltpu.make_async_remote_copy(
                        src_ref=kv_blocks.at[ch, s * mp_n + m],
                        dst_ref=grad_blocks.at[ch, my_c, my_m],
                        send_sem=grad_send.at[ch, s],
                        recv_sem=grad_recv.at[ch, my_c],
                        device_id=(s, m),
                        device_id_type=MESH,
                    ).start()

                if i > 0:
                    away()
                else:
                    pl.when(s != my_c)(away)

                    @pl.when(s == my_c)
                    def _():
                        pltpu.make_async_copy(
                            kv_blocks.at[ch, owner],
                            grad_blocks.at[ch, my_c, my_m],
                            grad_recv.at[ch, my_c],
                        ).start()

        loop(0, my_c + 1, to_owners)

    loop(0, chunks, work_chunk)

    dk_ref[...] = jnp.zeros(dk_ref.shape, jnp.float32)
    dv_ref[...] = jnp.zeros(dv_ref.shape, jnp.float32)

    def absorb_chunk(ch):
        def from_stretch(c):
            wait_bytes(grad_blocks.at[ch, c], grad_recv.at[ch, c])
            wanted = [hits[b, pl.ds(c, 1), :] for b in range(per_owner)]
            for m in range(mp_n):
                cols = columns(m, ch)
                for part, target in enumerate((dk_ref, dv_ref)):
                    grad = grad_blocks[ch, c, m, part].astype(jnp.float32)
                    for b in range(per_owner):
                        target[b * BLK : (b + 1) * BLK, cols] += grad * wanted[b]

        loop(my_c, ctx_n, from_stretch)

    loop(0, chunks, absorb_chunk)

    loop(0, my_c, lambda c: wait_bytes(list_ref, list_send.at[c]))

    def finish(ch):
        loop(my_c + 1, ctx_n, lambda c: wait_bytes(out_blocks.at[ch, c], kv_send.at[ch, c]))
        wait_bytes(out_blocks.at[ch, my_c, pl.ds(0, mp_n - 1)], kv_send.at[ch, my_c])
        loop(
            0,
            my_c,
            lambda s: wait_bytes(
                kv_blocks.at[ch, pl.ds(s * mp_n, mp_n)], grad_send.at[ch, s]
            ),
        )
        wait_bytes(kv_blocks.at[ch, pl.ds(my_c * mp_n, mp_n - 1)], grad_send.at[ch, my_c])

    loop(0, chunks, finish)


def store(*refs):
    half = len(refs) // 2
    sems, refs = refs[-1], refs[:-1]
    copies = [
        pltpu.make_async_copy(a, b, sems.at[i])
        for i, (a, b) in enumerate(zip(refs[:half], refs[half:]))
    ]
    for copy in copies:
        copy.start()
    for copy in copies:
        copy.wait()


def on_device(queries, cache_keys, cache_values, douts, reads):
    layers, tok, head_width = queries.shape
    kv_rows, full_width = cache_keys.shape
    ctx_n = lax.axis_size("ctx")
    mp_n = lax.axis_size("mp")
    per_owner = kv_rows // BLK
    owners = ctx_n * mp_n
    heads = head_width // HD
    chunks = heads
    width = HD
    slots = reads.shape[1]
    padded = -(-slots // LANES) * LANES
    vmem = pl.BlockSpec(memory_space=pltpu.VMEM)
    dma = pltpu.SemaphoreType.DMA
    results = pl.pallas_call(
        functools.partial(kernel, (ctx_n, mp_n, chunks, width)),
        out_shape=(
            jax.ShapeDtypeStruct(queries.shape, jnp.bfloat16),
            jax.ShapeDtypeStruct(queries.shape, jnp.bfloat16),
            jax.ShapeDtypeStruct(cache_keys.shape, jnp.float32),
            jax.ShapeDtypeStruct(cache_values.shape, jnp.float32),
        ),
        in_specs=[vmem] * 5,
        out_specs=(vmem,) * 4,
        scratch_shapes=[
            pltpu.VMEM((chunks, ctx_n, mp_n, 2, BLK, width), jnp.bfloat16),
            pltpu.VMEM((chunks, owners, 2, BLK, width), jnp.bfloat16),
            pltpu.VMEM((chunks, ctx_n, mp_n, 2, BLK, width), jnp.bfloat16),
            pltpu.VMEM((8, padded), jnp.int32),
            pltpu.VMEM((ctx_n, 8, padded), jnp.int32),
            pltpu.VMEM((per_owner, ctx_n, width), jnp.float32),
            pltpu.VMEM((tok, owners * BLK), jnp.float32),
            dma((ctx_n,)),
            dma((ctx_n,)),
            dma((chunks, ctx_n)),
            dma((chunks, ctx_n)),
            dma((chunks, ctx_n)),
            dma((chunks, ctx_n)),
        ],
        compiler_params=pltpu.CompilerParams(
            collective_id=0, has_side_effects=True, vmem_limit_bytes=60 * 1024 * 1024
        ),
    )(queries, cache_keys, cache_values, douts, reads)
    anywhere = pl.BlockSpec(memory_space=pl.ANY)
    return pl.pallas_call(
        store,
        out_shape=[jax.ShapeDtypeStruct(r.shape, r.dtype) for r in results],
        in_specs=[vmem] * 4,
        out_specs=[anywhere] * 4,
        scratch_shapes=[dma((4,))],
        compiler_params=pltpu.CompilerParams(vmem_limit_bytes=16 * 1024 * 1024),
    )(*results)


def solution(mesh):
    return jax.shard_map(
        on_device,
        mesh=mesh,
        in_specs=(
            P(None, "ctx", "mp"),
            P(("ctx", "mp"), None),
            P(("ctx", "mp"), None),
            P(None, "ctx", "mp"),
            P("ctx", None),
        ),
        out_specs=(
            P(None, "ctx", "mp"),
            P(None, "ctx", "mp"),
            P(("ctx", "mp"), None),
            P(("ctx", "mp"), None),
        ),
        check_vma=False,
    )
```
